32 devices in a mesh: groups: 2 (over y), outer: 2 (over core), inner: 8 (over z, x).
Axes of the slice: x: 2, y: 2, z: 4, core: 2. Of those that a mesh axis runs over, the one named last changes fastest.
Arguments:
- queries: bfloat16 [8192, 2048], P(('groups', 'outer', 'inner')), parts along dimension 0, may hold values from -120 to 120
- key_value: bfloat16 [2, 8192, 2048], P(None, ('groups', 'outer', 'inner')), parts along dimension 1, may hold values from -6 to 6
- region_table: int32 [16, 8], P('groups'), parts along dimension 0, may hold values from 0 to 15, as said below
- region_bias: float32 [16, 16], replicated, may hold values from -4 to 4
Outputs:
- attended: bfloat16 [8192, 2048], P(('groups', 'outer', 'inner')), parts along dimension 0
The draws below stay inside these ranges and needn't reach their ends.
There are 2 independent parts, one for each index of `groups`. The reference program is written for one: setup_inputs(seed, part) draws one part's arguments, and reference() takes and returns one part's arrays. A program takes and returns all parts, laid end to end along the dimension named above; an argument that names none is the same for every part. Nothing has to cross between parts.
Inputs may be any that keep to these rules, and one draw needn't show every extreme that they name: region_table[i, j] is 0 whenever |i - j| > 1, and region_table[i, i] >= 1.
All inputs are finite; a program needn't handle non-finite values.
Results may differ from the reference program's by a relative error of at most 0.0046.
Values may be sent and summed in bfloat16 or wider, within the bound.
A program may use at most 128 MiB of HBM per device.

```python
import math
import jax
import jax.numpy as jnp
from jax import lax

HEADS = 16
BLOCK = 512
REGIONS = 16
SEQ = 4096
NB = 8
FEAT = 2048


def make_fields(key):
    base_keys = jnp.clip(jax.random.normal(jax.random.fold_in(key, 12), (SEQ, FEAT), jnp.float32), -6.0, 6.0)
    base_values = jnp.clip(jax.random.normal(jax.random.fold_in(key, 13), (SEQ, FEAT), jnp.float32), -6.0, 6.0)
    final_queries = jnp.clip(jax.random.normal(jax.random.fold_in(key, 11), (SEQ, FEAT), jnp.float32), -6.0, 6.0)
    final_keys = base_keys
    return (final_queries, final_keys, base_values)


def draw_queries(key, part):
    final_queries, final_keys, final_values = make_fields(key)
    return final_queries.astype(jnp.bfloat16)


def draw_key_value(key, part):
    final_queries, final_keys, final_values = make_fields(key)
    return jnp.stack([final_keys, final_values]).astype(jnp.bfloat16)


def draw_region_table(key, part):
    row_index = jnp.arange(NB)[:, None]
    col_index = jnp.arange(NB)[None, :]
    region_ids = jax.random.randint(jax.random.fold_in(key, 21), (NB, NB), 1, REGIONS)
    row_density = jax.random.randint(jax.random.fold_in(key, 22), (NB, 1), 0, 5)
    trial_draw = jax.random.randint(jax.random.fold_in(key, 23), (NB, NB), 0, 4)
    live_pairs = (row_index == col_index) | (jnp.abs(row_index - col_index) == 1) & (trial_draw < row_density)
    return jnp.where(live_pairs, region_ids, 0).astype(jnp.int32)


def normal_values(own_key, shape, width, reach, held_as=jnp.bfloat16):
    return jnp.clip(width * jax.random.normal(own_key, shape, jnp.float32), -reach, reach).astype(held_as)


def setup_inputs(seed: int = 0, part: int = 0) -> dict:
    arg_keys = jax.random.split(jax.random.key(seed), 5)
    part_splits = jax.random.split(jax.random.fold_in(arg_keys[4], part), 5)
    queries = draw_queries(jax.random.fold_in(jax.random.fold_in(arg_keys[4], part), 71), part)
    key_value = draw_key_value(jax.random.fold_in(jax.random.fold_in(arg_keys[4], part), 71), part)
    region_table = draw_region_table(jax.random.fold_in(jax.random.fold_in(arg_keys[4], part), 71), part)
    region_bias = normal_values(arg_keys[3], (HEADS, REGIONS), 1.0, 4.0, jnp.float32)
    return dict(queries=queries, key_value=key_value, region_table=region_table, region_bias=region_bias)


def reference(queries, key_value, region_table, region_bias):
    sequence, feature_width = queries.shape
    head_count = region_bias.shape[0]
    head_size = feature_width // head_count
    block_count = sequence // BLOCK
    score_scale = 1.0 / math.sqrt(head_size)
    keys_padded = jnp.pad(key_value[0], ((BLOCK, BLOCK), (0, 0)))
    values_padded = jnp.pad(key_value[1], ((BLOCK, BLOCK), (0, 0)))
    table_padded = jnp.pad(region_table, ((0, 0), (1, 1)))
    regions = jnp.arange(REGIONS, dtype=jnp.int32)

    def attend_block(block_index):
        row_start = (block_index * BLOCK).astype(jnp.int32)
        query_rows = lax.dynamic_slice_in_dim(queries, row_start, BLOCK, 0).astype(jnp.float32).reshape(BLOCK, head_count, head_size)
        key_rows = lax.dynamic_slice_in_dim(keys_padded, row_start, 3 * BLOCK, 0).astype(jnp.float32).reshape(3 * BLOCK, head_count, head_size)
        value_rows = lax.dynamic_slice_in_dim(values_padded, row_start, 3 * BLOCK, 0).astype(jnp.float32).reshape(3 * BLOCK, head_count, head_size)
        region_ids = lax.dynamic_slice(table_padded, (block_index.astype(jnp.int32), block_index.astype(jnp.int32)), (1, 3))[0]
        one_hot = (region_ids[:, None] == regions[None, :]).astype(jnp.float32)
        bias_blocks = jnp.dot(region_bias, one_hot.T, precision=lax.Precision.HIGHEST)
        bias_keys = jnp.repeat(bias_blocks, BLOCK, axis=1)
        live_keys = jnp.repeat(region_ids > 0, BLOCK)
        scores = jnp.einsum('thd,uhd->htu', query_rows, key_rows) * score_scale + bias_keys[:, None, :]
        scores = jnp.where(live_keys[None, None, :], scores, -1e+30)
        row_peak = lax.optimization_barrier(jnp.max(scores, axis=-1, keepdims=True))
        weights = jnp.exp(scores - row_peak)
        row_total = lax.optimization_barrier(jnp.sum(weights, axis=-1))
        rounded = lax.optimization_barrier(weights.astype(jnp.bfloat16)).astype(jnp.float32)
        weighted = jnp.einsum('htu,uhd->thd', rounded, value_rows)
        attended = weighted / row_total.T[:, :, None]
        return attended.reshape(BLOCK, feature_width).astype(jnp.bfloat16)
    blocks_out = lax.map(attend_block, jnp.arange(block_count, dtype=jnp.int32))
    return blocks_out.reshape(sequence, feature_width)
```

```python
import functools
import math

import jax
import jax.numpy as jnp
from jax import lax
from jax.experimental import pallas as pl
from jax.experimental.pallas import tpu as pltpu
from jax.sharding import PartitionSpec as P

MESH = pl.DeviceIdType.MESH
BELOW, OWN, ABOVE = 0, 1, 2
LOG2E = math.log2(math.e)
DEAD = -1e30


def kernel(
    inner,
    positions,
    table_ref,
    bias_ref,
    q_ref,
    kv_ref,
    out_ref,
    q_buf,
    kv_buf,
    o_buf,
    q_local,
    kv_local,
    o_local,
    q_send,
    q_recv,
    kv_send,
    kv_recv,
    z_send,
    z_recv,
    o_send,
    o_recv,
):
    heads, _, _, block, head_size = kv_buf.shape
    rows = block // 2
    group = lax.axis_index("groups")
    position = lax.axis_index("outer") * inner + lax.axis_index("inner")
    side = lax.rem(position, 2)
    has_below = position >= 2
    has_above = position < positions - 2

    def at(where):
        return (group, where // inner, lax.rem(where, inner))

    partner = at(position + 1 - 2 * side)
    below = at(jnp.maximum(position - 2, 0))
    above = at(jnp.minimum(position + 2, positions - 1))
    own_rows = pl.ds(pl.multiple_of(side * rows, rows), rows)
    partner_rows = pl.ds(pl.multiple_of((1 - side) * rows, rows), rows)

    def columns(which_side, head):
        return pl.ds(pl.multiple_of((which_side * heads + head) * head_size, head_size), head_size)

    def remote(src, dst, send, recv, target):
        return pltpu.make_async_remote_copy(
            src_ref=src, dst_ref=dst, send_sem=send, recv_sem=recv, device_id=target, device_id_type=MESH
        )

    def q_pair(head, which_rows):
        return remote(
            q_ref.at[:, columns(1 - side, head)],
            q_buf.at[head, which_rows],
            q_send.at[head],
            q_recv.at[head],
            partner,
        )

    def kv_pair(head, which_rows):
        return remote(
            kv_ref.at[:, :, columns(1 - side, head)],
            kv_buf.at[head, OWN, :, which_rows],
            kv_send.at[head],
            kv_recv.at[head],
            partner,
        )

    def q_keep(head):
        return pltpu.make_async_copy(
            q_ref.at[:, columns(side, head)], q_buf.at[head, own_rows], q_local.at[head]
        )

    def kv_keep(head):
        return pltpu.make_async_copy(
            kv_ref.at[:, :, columns(side, head)], kv_buf.at[head, OWN, :, own_rows], kv_local.at[head]
        )

    def own_along(head, up):
        return remote(
            kv_ref.at[:, :, columns(side, head)],
            kv_buf.at[head, BELOW if up else ABOVE, :, own_rows],
            z_send.at[int(up), 0, head],
            z_recv.at[int(up), 0, head],
            above if up else below,
        )

    def passed_along(head, up):
        return remote(
            kv_buf.at[head, OWN, :, partner_rows],
            kv_buf.at[head, BELOW if up else ABOVE, :, partner_rows],
            z_send.at[int(up), 1, head],
            z_recv.at[int(up), 1, head],
            above if up else below,
        )

    def out_pair(head, which_side):
        return remote(
            o_buf.at[head, partner_rows],
            out_ref.at[:, columns(which_side, head)],
            o_send.at[head],
            o_recv.at[head],
            partner,
        )

    def out_keep(head):
        return pltpu.make_async_copy(
            o_buf.at[head, own_rows], out_ref.at[:, columns(side, head)], o_local.at[head]
        )

    def each_head(body):
        lax.fori_loop(0, heads, lambda head, carry: (body(head), carry)[1], 0)

    barrier = pltpu.get_barrier_semaphore()
    pl.semaphore_signal(barrier, inc=1, device_id=partner, device_id_type=MESH)

    @pl.when(has_below)
    def _():
        pl.semaphore_signal(barrier, inc=1, device_id=below, device_id_type=MESH)

    @pl.when(has_above)
    def _():
        pl.semaphore_signal(barrier, inc=1, device_id=above, device_id_type=MESH)

    pl.semaphore_wait(barrier, 1 + has_below.astype(jnp.int32) + has_above.astype(jnp.int32))

    def start_first(head):
        kv_pair(head, own_rows).start()

        @pl.when(has_above)
        def _():
            own_along(head, True).start()

        @pl.when(has_below)
        def _():
            own_along(head, False).start()

    each_head(start_first)

    def start_second(head):
        q_pair(head, own_rows).start()
        q_keep(head).start()
        kv_keep(head).start()

    each_head(start_second)

    @pl.when(jnp.logical_not(has_below))
    def _():
        each_head(lambda head: kv_buf.__setitem__((head, BELOW), jnp.zeros((2, block, head_size), kv_buf.dtype)))

    @pl.when(jnp.logical_not(has_above))
    def _():
        each_head(lambda head: kv_buf.__setitem__((head, ABOVE), jnp.zeros((2, block, head_size), kv_buf.dtype)))

    def pass_on(head):
        kv_pair(head, partner_rows).wait_recv()

        @pl.when(has_above)
        def _():
            passed_along(head, True).start()

        @pl.when(has_below)
        def _():
            passed_along(head, False).start()

    each_head(pass_on)

    block_index = position // 2
    last_block = positions // 2 - 1
    scale = LOG2E / math.sqrt(head_size)

    def key_bias(head, slot):
        key_block = jnp.clip(block_index + slot - 1, 0, last_block)
        region = table_ref[block_index, key_block]
        live = region > 0
        if slot == BELOW:
            live = live & has_below
        if slot == ABOVE:
            live = live & has_above
        return jnp.where(live, bias_ref[side * heads + head, region] * LOG2E, DEAD)

    def attend(head):
        q_pair(head, partner_rows).wait_recv()
        q_keep(head).wait()
        kv_keep(head).wait()

        @pl.when(has_below)
        def _():
            own_along(head, True).wait_recv()
            passed_along(head, True).wait_recv()

        @pl.when(has_above)
        def _():
            own_along(head, False).wait_recv()
            passed_along(head, False).wait_recv()

        biases = [key_bias(head, slot) for slot in (BELOW, OWN, ABOVE)]
        for half in range(2):
            tile = pl.ds(half * rows, rows)
            query = q_buf[head, tile]
            products = [
                lax.dot_general(
                    query, kv_buf[head, slot, 0], (((1,), (1,)), ((), ())), preferred_element_type=jnp.float32
                )
                for slot in (BELOW, OWN, ABOVE)
            ]
            peak = functools.reduce(
                jnp.maximum,
                [jnp.max(tile_, axis=1, keepdims=True) * scale + bias for tile_, bias in zip(products, biases)],
            )
            total = jnp.zeros((rows, 1), jnp.float32)
            weighted = jnp.zeros((rows, head_size), jnp.float32)
            for slot in (BELOW, OWN, ABOVE):
                weights = jnp.exp2(products[slot] * scale + (biases[slot] - peak))
                total = total + jnp.sum(weights, axis=1, keepdims=True)
                weighted = weighted + jnp.dot(
                    weights.astype(jnp.bfloat16), kv_buf[head, slot, 1], preferred_element_type=jnp.float32
                )
            o_buf[head, tile] = (weighted / total).astype(o_buf.dtype)
        out_pair(head, side).start()
        out_keep(head).start()

    each_head(attend)

    def finish(head):
        out_keep(head).wait()
        out_pair(head, side).wait_send()
        out_pair(head, 1 - side).wait_recv()
        q_pair(head, own_rows).wait_send()
        kv_pair(head, own_rows).wait_send()

        @pl.when(has_above)
        def _():
            own_along(head, True).wait_send()
            passed_along(head, True).wait_send()

        @pl.when(has_below)
        def _():
            own_along(head, False).wait_send()
            passed_along(head, False).wait_send()

    each_head(finish)


def per_device(inner, positions, queries, key_value, region_table, region_bias):
    tokens, feature_width = queries.shape
    head_count = region_bias.shape[0]
    head_size = feature_width // head_count
    heads = head_count // 2
    block = 2 * tokens
    dma = pltpu.SemaphoreType.DMA
    return pl.pallas_call(
        functools.partial(kernel, inner, positions),
        out_shape=jax.ShapeDtypeStruct((tokens, feature_width), jnp.bfloat16),
        in_specs=[
            pl.BlockSpec(memory_space=pltpu.SMEM),
            pl.BlockSpec(memory_space=pltpu.SMEM),
            pl.BlockSpec(memory_space=pl.ANY),
            pl.BlockSpec(memory_space=pl.ANY),
        ],
        out_specs=pl.BlockSpec(memory_space=pl.ANY),
        scratch_shapes=[
            pltpu.VMEM((heads, block, head_size), jnp.bfloat16),
            pltpu.VMEM((heads, 3, 2, block, head_size), jnp.bfloat16),
            pltpu.VMEM((heads, block, head_size), jnp.bfloat16),
            dma((heads,)),
            dma((heads,)),
            dma((heads,)),
            dma((heads,)),
            dma((heads,)),
            dma((heads,)),
            dma((heads,)),
            dma((2, 2, heads)),
            dma((2, 2, heads)),
            dma((heads,)),
            dma((heads,)),
        ],
        compiler_params=pltpu.CompilerParams(
            collective_id=0, has_side_effects=True, vmem_limit_bytes=48 * 1024 * 1024
        ),
    )(region_table, region_bias, queries, key_value)


def solution(mesh):
    inner = mesh.shape["inner"]
    positions = mesh.shape["outer"] * inner
    placed = (
        P(("groups", "outer", "inner"), None),
        P(None, ("groups", "outer", "inner"), None),
        P("groups", None),
        P(),
    )
    return jax.shard_map(
        functools.partial(per_device, inner, positions),
        mesh=mesh,
        in_specs=placed,
        out_specs=P(("groups", "outer", "inner"), None),
        check_vma=False,
    )
```

```python
import functools
import math

import jax
import jax.numpy as jnp
from jax import lax
from jax.experimental import pallas as pl
from jax.experimental.pallas import tpu as pltpu
from jax.sharding import PartitionSpec as P

MESH = pl.DeviceIdType.MESH
BELOW, OWN, ABOVE = 0, 1, 2
LOG2E = math.log2(math.e)
DEAD = -1e30
ALONG_AHEAD = 2
PAIR_AHEAD = 4


def kernel(
    inner,
    positions,
    table_hbm,
    bias_hbm,
    q_ref,
    kv_ref,
    out_ref,
    table_ref,
    bias_ref,
    q_buf,
    kv_buf,
    o_buf,
    table_local,
    bias_local,
    q_local,
    kv_local,
    o_local,
    q_send,
    q_recv,
    kv_send,
    kv_recv,
    z_send,
    z_recv,
    o_send,
    o_recv,
):
    heads, _, _, block, head_size = kv_buf.shape
    rows = block // 2
    group = lax.axis_index("groups")
    position = lax.axis_index("outer") * inner + lax.axis_index("inner")
    side = lax.rem(position, 2)
    has_below = position >= 2
    has_above = position < positions - 2

    def at(where):
        return (group, where // inner, lax.rem(where, inner))

    partner = at(position + 1 - 2 * side)
    below = at(jnp.maximum(position - 2, 0))
    above = at(jnp.minimum(position + 2, positions - 1))
    own_rows = pl.ds(pl.multiple_of(side * rows, rows), rows)
    partner_rows = pl.ds(pl.multiple_of((1 - side) * rows, rows), rows)

    def columns(which_side, head):
        return pl.ds(pl.multiple_of((which_side * heads + head) * head_size, head_size), head_size)

    def remote(src, dst, send, recv, target):
        return pltpu.make_async_remote_copy(
            src_ref=src, dst_ref=dst, send_sem=send, recv_sem=recv, device_id=target, device_id_type=MESH
        )

    def q_pair(head, which_rows):
        return remote(
            q_ref.at[:, columns(1 - side, head)],
            q_buf.at[head, which_rows],
            q_send.at[head],
            q_recv.at[head],
            partner,
        )

    def kv_pair(head, which_rows):
        return remote(
            kv_ref.at[:, :, columns(1 - side, head)],
            kv_buf.at[head, OWN, :, which_rows],
            kv_send.at[head],
            kv_recv.at[head],
            partner,
        )

    def q_keep(head):
        return pltpu.make_async_copy(
            q_ref.at[:, columns(side, head)], q_buf.at[head, own_rows], q_local.at[head]
        )

    def kv_keep(head):
        return pltpu.make_async_copy(
            kv_ref.at[:, :, columns(side, head)], kv_buf.at[head, OWN, :, own_rows], kv_local.at[head]
        )

    def own_along(head, up):
        return remote(
            kv_ref.at[:, :, columns(side, head)],
            kv_buf.at[head, BELOW if up else ABOVE, :, own_rows],
            z_send.at[int(up), 0, head],
            z_recv.at[int(up), 0, head],
            above if up else below,
        )

    def passed_along(head, up):
        return remote(
            kv_buf.at[head, OWN, :, partner_rows],
            kv_buf.at[head, BELOW if up else ABOVE, :, partner_rows],
            z_send.at[int(up), 1, head],
            z_recv.at[int(up), 1, head],
            above if up else below,
        )

    def out_pair(head, which_side):
        return remote(
            o_buf.at[head, partner_rows],
            out_ref.at[:, columns(which_side, head)],
            o_send.at[head],
            o_recv.at[head],
            partner,
        )

    def out_keep(head):
        return pltpu.make_async_copy(
            o_buf.at[head, own_rows], out_ref.at[:, columns(side, head)], o_local.at[head]
        )

    def each_head(body):
        lax.fori_loop(0, heads, lambda head, carry: (body(head), carry)[1], 0)

    table_keep = pltpu.make_async_copy(table_hbm, table_ref, table_local)
    bias_keep = pltpu.make_async_copy(bias_hbm, bias_ref, bias_local)
    table_keep.start()
    bias_keep.start()

    barrier = pltpu.get_barrier_semaphore()
    pl.semaphore_signal(barrier, inc=1, device_id=partner, device_id_type=MESH)

    @pl.when(has_below)
    def _():
        pl.semaphore_signal(barrier, inc=1, device_id=below, device_id_type=MESH)

    @pl.when(has_above)
    def _():
        pl.semaphore_signal(barrier, inc=1, device_id=above, device_id_type=MESH)

    pl.semaphore_wait(barrier, 1 + has_below.astype(jnp.int32) + has_above.astype(jnp.int32))

    def start_pair(head):
        kv_pair(head, own_rows).start()
        q_pair(head, own_rows).start()

    def start_own(head):
        @pl.when(has_above)
        def _():
            own_along(head, True).start()

        @pl.when(has_below)
        def _():
            own_along(head, False).start()

    def start_passed(head):
        kv_pair(head, partner_rows).wait_recv()

        @pl.when(has_above)
        def _():
            passed_along(head, True).start()

        @pl.when(has_below)
        def _():
            passed_along(head, False).start()

    def start_keep(head):
        q_keep(head).start()
        kv_keep(head).start()

    for head in range(PAIR_AHEAD):
        start_pair(head)
        if head < ALONG_AHEAD:
            start_own(head)
    each_head(start_keep)

    @pl.when(jnp.logical_not(has_below))
    def _():
        each_head(lambda head: kv_buf.__setitem__((head, BELOW), jnp.zeros((2, block, head_size), kv_buf.dtype)))

    @pl.when(jnp.logical_not(has_above))
    def _():
        each_head(lambda head: kv_buf.__setitem__((head, ABOVE), jnp.zeros((2, block, head_size), kv_buf.dtype)))

    for head in range(ALONG_AHEAD):
        start_passed(head)
    table_keep.wait()
    bias_keep.wait()

    block_index = position // 2
    last_block = positions // 2 - 1
    scale = LOG2E / math.sqrt(head_size)

    def key_bias(head, slot):
        key_block = jnp.clip(block_index + slot - 1, 0, last_block)
        region = table_ref[block_index, key_block]
        live = region > 0
        if slot == BELOW:
            live = live & has_below
        if slot == ABOVE:
            live = live & has_above
        return jnp.where(live, bias_ref[side * heads + head, region] * LOG2E, DEAD)

    def attend(head):
        q_pair(head, partner_rows).wait_recv()
        q_keep(head).wait()
        kv_keep(head).wait()

        @pl.when(has_below)
        def _():
            own_along(head, True).wait_recv()
            passed_along(head, True).wait_recv()

        @pl.when(has_above)
        def _():
            own_along(head, False).wait_recv()
            passed_along(head, False).wait_recv()

        @pl.when(head + ALONG_AHEAD < heads)
        def _():
            start_own(head + ALONG_AHEAD)
            start_passed(head + ALONG_AHEAD)

        @pl.when(head + PAIR_AHEAD < heads)
        def _():
            start_pair(head + PAIR_AHEAD)

        biases = [key_bias(head, slot) for slot in (BELOW, OWN, ABOVE)]
        for half in range(2):
            tile = pl.ds(half * rows, rows)
            query = q_buf[head, tile]
            products = [
                lax.dot_general(
                    query, kv_buf[head, slot, 0], (((1,), (1,)), ((), ())), preferred_element_type=jnp.float32
                )
                for slot in (BELOW, OWN, ABOVE)
            ]
            peak = functools.reduce(
                jnp.maximum,
                [jnp.max(tile_, axis=1, keepdims=True) * scale + bias for tile_, bias in zip(products, biases)],
            )
            total = jnp.zeros((rows, 1), jnp.float32)
            weighted = jnp.zeros((rows, head_size), jnp.float32)
            for slot in (BELOW, OWN, ABOVE):
                weights = jnp.exp2(products[slot] * scale + (biases[slot] - peak))
                total = total + jnp.sum(weights, axis=1, keepdims=True)
                weighted = weighted + jnp.dot(
                    weights.astype(jnp.bfloat16), kv_buf[head, slot, 1], preferred_element_type=jnp.float32
                )
            o_buf[head, tile] = (weighted / total).astype(o_buf.dtype)
        out_pair(head, side).start()
        out_keep(head).start()

    each_head(attend)

    def finish(head):
        out_keep(head).wait()
        out_pair(head, side).wait_send()
        out_pair(head, 1 - side).wait_recv()
        q_pair(head, own_rows).wait_send()
        kv_pair(head, own_rows).wait_send()

        @pl.when(has_above)
        def _():
            own_along(head, True).wait_send()
            passed_along(head, True).wait_send()

        @pl.when(has_below)
        def _():
            own_along(head, False).wait_send()
            passed_along(head, False).wait_send()

    each_head(finish)


def per_device(inner, positions, queries, key_value, region_table, region_bias):
    tokens, feature_width = queries.shape
    head_count = region_bias.shape[0]
    head_size = feature_width // head_count
    heads = head_count // 2
    block = 2 * tokens
    dma = pltpu.SemaphoreType.DMA
    return pl.pallas_call(
        functools.partial(kernel, inner, positions),
        out_shape=jax.ShapeDtypeStruct((tokens, feature_width), jnp.bfloat16),
        in_specs=[
            pl.BlockSpec(memory_space=pl.ANY),
            pl.BlockSpec(memory_space=pl.ANY),
            pl.BlockSpec(memory_space=pl.ANY),
            pl.BlockSpec(memory_space=pl.ANY),
        ],
        out_specs=pl.BlockSpec(memory_space=pl.ANY),
        scratch_shapes=[
            pltpu.SMEM(region_table.shape, region_table.dtype),
            pltpu.SMEM(region_bias.shape, region_bias.dtype),
            pltpu.VMEM((heads, block, head_size), jnp.bfloat16),
            pltpu.VMEM((heads, 3, 2, block, head_size), jnp.bfloat16),
            pltpu.VMEM((heads, block, head_size), jnp.bfloat16),
            dma,
            dma,
            dma((heads,)),
            dma((heads,)),
            dma((heads,)),
            dma((heads,)),
            dma((heads,)),
            dma((heads,)),
            dma((heads,)),
            dma((2, 2, heads)),
            dma((2, 2, heads)),
            dma((heads,)),
            dma((heads,)),
        ],
        compiler_params=pltpu.CompilerParams(
            collective_id=0, has_side_effects=True, vmem_limit_bytes=60 * 1024 * 1024
        ),
    )(region_table, region_bias, queries, key_value)


def solution(mesh):
    inner = mesh.shape["inner"]
    positions = mesh.shape["outer"] * inner
    placed = (
        P(("groups", "outer", "inner"), None),
        P(None, ("groups", "outer", "inner"), None),
        P("groups", None),
        P(),
    )
    return jax.shard_map(
        functools.partial(per_device, inner, positions),
        mesh=mesh,
        in_specs=placed,
        out_specs=P(("groups", "outer", "inner"), None),
        check_vma=False,
    )
```

```python
import functools
import math

import jax
import jax.numpy as jnp
from jax import lax
from jax.experimental import pallas as pl
from jax.experimental.pallas import tpu as pltpu
from jax.sharding import PartitionSpec as P

MESH = pl.DeviceIdType.MESH
BELOW, OWN, ABOVE = 0, 1, 2
LOG2E = math.log2(math.e)
DEAD = -1e30
ALONG_AHEAD = 2
PAIR_AHEAD = 4


def kernel(
    inner,
    positions,
    table_hbm,
    bias_hbm,
    q_ref,
    kv_ref,
    out_ref,
    table_ref,
    bias_ref,
    q_buf,
    kv_buf,
    o_buf,
    w_buf,
    table_local,
    bias_local,
    q_local,
    kv_local,
    o_local,
    q_send,
    q_recv,
    kv_send,
    kv_recv,
    z_send,
    z_recv,
    o_send,
    o_recv,
):
    heads, _, _, block, head_size = kv_buf.shape
    rows = block // 2
    group = lax.axis_index("groups")
    position = lax.axis_index("outer") * inner + lax.axis_index("inner")
    side = lax.rem(position, 2)
    has_below = position >= 2
    has_above = position < positions - 2

    def at(where):
        return (group, where // inner, lax.rem(where, inner))

    partner = at(position + 1 - 2 * side)
    below = at(jnp.maximum(position - 2, 0))
    above = at(jnp.minimum(position + 2, positions - 1))
    own_rows = pl.ds(pl.multiple_of(side * rows, rows), rows)
    partner_rows = pl.ds(pl.multiple_of((1 - side) * rows, rows), rows)

    def columns(which_side, head):
        return pl.ds(pl.multiple_of((which_side * heads + head) * head_size, head_size), head_size)

    def remote(src, dst, send, recv, target):
        return pltpu.make_async_remote_copy(
            src_ref=src, dst_ref=dst, send_sem=send, recv_sem=recv, device_id=target, device_id_type=MESH
        )

    def q_pair(head, which_rows):
        return remote(
            q_ref.at[:, columns(1 - side, head)],
            q_buf.at[head, which_rows],
            q_send.at[head],
            q_recv.at[head],
            partner,
        )

    def kv_pair(head, which_rows):
        return remote(
            kv_ref.at[:, :, columns(1 - side, head)],
            kv_buf.at[head, OWN, :, which_rows],
            kv_send.at[head],
            kv_recv.at[head],
            partner,
        )

    def q_keep(head):
        return pltpu.make_async_copy(
            q_ref.at[:, columns(side, head)], q_buf.at[head, own_rows], q_local.at[head]
        )

    def kv_keep(head):
        return pltpu.make_async_copy(
            kv_ref.at[:, :, columns(side, head)], kv_buf.at[head, OWN, :, own_rows], kv_local.at[head]
        )

    def own_along(head, part, up):
        return remote(
            kv_ref.at[part, :, columns(side, head)],
            kv_buf.at[head, BELOW if up else ABOVE, part, own_rows],
            z_send.at[int(up), 0, part, head],
            z_recv.at[int(up), 0, part, head],
            above if up else below,
        )

    def passed_along(head, part, up):
        return remote(
            kv_buf.at[head, OWN, part, partner_rows],
            kv_buf.at[head, BELOW if up else ABOVE, part, partner_rows],
            z_send.at[int(up), 1, part, head],
            z_recv.at[int(up), 1, part, head],
            above if up else below,
        )

    def both_ways(act):
        @pl.when(has_above)
        def _():
            act(True)

        @pl.when(has_below)
        def _():
            act(False)

    def wait_along(head, part):
        @pl.when(has_below)
        def _():
            own_along(head, part, True).wait_recv()
            passed_along(head, part, True).wait_recv()

        @pl.when(has_above)
        def _():
            own_along(head, part, False).wait_recv()
            passed_along(head, part, False).wait_recv()

    def out_pair(head, which_side):
        return remote(
            o_buf.at[head, partner_rows],
            out_ref.at[:, columns(which_side, head)],
            o_send.at[head],
            o_recv.at[head],
            partner,
        )

    def out_keep(head):
        return pltpu.make_async_copy(
            o_buf.at[head, own_rows], out_ref.at[:, columns(side, head)], o_local.at[head]
        )

    def each_head(body):
        lax.fori_loop(0, heads, lambda head, carry: (body(head), carry)[1], 0)

    barrier = pltpu.get_barrier_semaphore()
    pl.semaphore_signal(barrier, inc=1, device_id=partner, device_id_type=MESH)

    @pl.when(has_below)
    def _():
        pl.semaphore_signal(barrier, inc=1, device_id=below, device_id_type=MESH)

    @pl.when(has_above)
    def _():
        pl.semaphore_signal(barrier, inc=1, device_id=above, device_id_type=MESH)

    table_keep = pltpu.make_async_copy(table_hbm, table_ref, table_local)
    bias_keep = pltpu.make_async_copy(bias_hbm, bias_ref, bias_local)
    table_keep.start()
    bias_keep.start()

    def start_keep(head):
        q_keep(head).start()
        kv_keep(head).start()

    each_head(start_keep)

    pl.semaphore_wait(barrier, 1 + has_below.astype(jnp.int32) + has_above.astype(jnp.int32))

    def start_pair(head):
        kv_pair(head, own_rows).start()
        q_pair(head, own_rows).start()

    def start_own(head, part):
        both_ways(lambda up: own_along(head, part, up).start())

    def start_passed(head, part):
        both_ways(lambda up: passed_along(head, part, up).start())

    for head in range(ALONG_AHEAD):
        start_own(head, 0)
        start_pair(head)
        start_own(head, 1)
    for head in range(ALONG_AHEAD, PAIR_AHEAD):
        start_pair(head)

    @pl.when(jnp.logical_not(has_below))
    def _():
        each_head(lambda head: kv_buf.__setitem__((head, BELOW), jnp.zeros((2, block, head_size), kv_buf.dtype)))

    @pl.when(jnp.logical_not(has_above))
    def _():
        each_head(lambda head: kv_buf.__setitem__((head, ABOVE), jnp.zeros((2, block, head_size), kv_buf.dtype)))

    for head in range(ALONG_AHEAD):
        kv_pair(head, partner_rows).wait_recv()
        start_passed(head, 0)
        start_passed(head, 1)
    table_keep.wait()
    bias_keep.wait()

    block_index = position // 2
    last_block = positions // 2 - 1
    scale = LOG2E / math.sqrt(head_size)

    def key_bias(head, slot):
        key_block = jnp.clip(block_index + slot - 1, 0, last_block)
        region = table_ref[block_index, key_block]
        live = region > 0
        if slot == BELOW:
            live = live & has_below
        if slot == ABOVE:
            live = live & has_above
        return jnp.where(live, bias_ref[side * heads + head, region] * LOG2E, DEAD)

    def attend(head):
        q_pair(head, partner_rows).wait_recv()
        q_keep(head).wait()
        kv_keep(head).wait()
        wait_along(head, 0)

        @pl.when(head + ALONG_AHEAD < heads)
        def _():
            kv_pair(head + ALONG_AHEAD, partner_rows).wait_recv()
            start_own(head + ALONG_AHEAD, 0)
            start_passed(head + ALONG_AHEAD, 0)
            start_own(head + ALONG_AHEAD, 1)
            start_passed(head + ALONG_AHEAD, 1)

        @pl.when(head + PAIR_AHEAD < heads)
        def _():
            start_pair(head + PAIR_AHEAD)

        slots = (BELOW, OWN, ABOVE)
        biases = [key_bias(head, slot) for slot in slots]
        totals = []
        for half, tile in enumerate((partner_rows, own_rows)):
            query = q_buf[head, tile]
            products = [
                lax.dot_general(
                    query, kv_buf[head, slot, 0], (((1,), (1,)), ((), ())), preferred_element_type=jnp.float32
                )
                for slot in slots
            ]
            peak = functools.reduce(
                jnp.maximum,
                [jnp.max(scores, axis=1, keepdims=True) * scale + bias for scores, bias in zip(products, biases)],
            )
            total = jnp.zeros((rows, 1), jnp.float32)
            for slot in slots:
                weights = jnp.exp2(products[slot] * scale + (biases[slot] - peak))
                total = total + jnp.sum(weights, axis=1, keepdims=True)
                w_buf[half, slot] = weights.astype(w_buf.dtype)
            totals.append(total)
        wait_along(head, 1)
        for half, tile in enumerate((partner_rows, own_rows)):
            weighted = jnp.zeros((rows, head_size), jnp.float32)
            for slot in slots:
                weighted = weighted + jnp.dot(
                    w_buf[half, slot], kv_buf[head, slot, 1], preferred_element_type=jnp.float32
                )
            o_buf[head, tile] = (weighted / totals[half]).astype(o_buf.dtype)
            if half == 0:
                out_pair(head, side).start()
        out_keep(head).start()

    each_head(attend)

    def finish_sends(head):
        q_pair(head, own_rows).wait_send()
        kv_pair(head, own_rows).wait_send()
        for part in range(2):
            both_ways(lambda up: own_along(head, part, up).wait_send())
            both_ways(lambda up: passed_along(head, part, up).wait_send())

    each_head(finish_sends)

    def finish(head):
        out_keep(head).wait()
        out_pair(head, side).wait_send()
        out_pair(head, 1 - side).wait_recv()

    each_head(finish)


def per_device(inner, positions, queries, key_value, region_table, region_bias):
    tokens, feature_width = queries.shape
    head_count = region_bias.shape[0]
    head_size = feature_width // head_count
    heads = head_count // 2
    block = 2 * tokens
    dma = pltpu.SemaphoreType.DMA
    return pl.pallas_call(
        functools.partial(kernel, inner, positions),
        out_shape=jax.ShapeDtypeStruct((tokens, feature_width), jnp.bfloat16),
        in_specs=[
            pl.BlockSpec(memory_space=pl.ANY),
            pl.BlockSpec(memory_space=pl.ANY),
            pl.BlockSpec(memory_space=pl.ANY),
            pl.BlockSpec(memory_space=pl.ANY),
        ],
        out_specs=pl.BlockSpec(memory_space=pl.ANY),
        scratch_shapes=[
            pltpu.SMEM(region_table.shape, region_table.dtype),
            pltpu.SMEM(region_bias.shape, region_bias.dtype),
            pltpu.VMEM((heads, block, head_size), jnp.bfloat16),
            pltpu.VMEM((heads, 3, 2, block, head_size), jnp.bfloat16),
            pltpu.VMEM((heads, block, head_size), jnp.bfloat16),
            pltpu.VMEM((2, 3, tokens, block), jnp.bfloat16),
            dma,
            dma,
            dma((heads,)),
            dma((heads,)),
            dma((heads,)),
            dma((heads,)),
            dma((heads,)),
            dma((heads,)),
            dma((heads,)),
            dma((2, 2, 2, heads)),
            dma((2, 2, 2, heads)),
            dma((heads,)),
            dma((heads,)),
        ],
        compiler_params=pltpu.CompilerParams(
            collective_id=0, has_side_effects=True, vmem_limit_bytes=60 * 1024 * 1024
        ),
    )(region_table, region_bias, queries, key_value)


def solution(mesh):
    inner = mesh.shape["inner"]
    positions = mesh.shape["outer"] * inner
    placed = (
        P(("groups", "outer", "inner"), None),
        P(None, ("groups", "outer", "inner"), None),
        P("groups", None),
        P(),
    )
    return jax.shard_map(
        functools.partial(per_device, inner, positions),
        mesh=mesh,
        in_specs=placed,
        out_specs=P(("groups", "outer", "inner"), None),
        check_vma=False,
    )
```

```python
import functools
import math

import jax
import jax.numpy as jnp
from jax import lax
from jax.experimental import pallas as pl
from jax.experimental.pallas import tpu as pltpu
from jax.sharding import PartitionSpec as P

MESH = pl.DeviceIdType.MESH
BELOW, OWN, ABOVE = 0, 1, 2
LOG2E = math.log2(math.e)
DEAD = -1e30
ALONG_AHEAD = 2
PAIR_AHEAD = 4
FINISH_BEHIND = 3


def kernel(
    inner,
    positions,
    table_hbm,
    bias_hbm,
    q_ref,
    kv_ref,
    out_ref,
    table_ref,
    bias_ref,
    q_buf,
    kv_buf,
    o_buf,
    w_buf,
    table_local,
    bias_local,
    q_local,
    kv_local,
    o_local,
    q_send,
    q_recv,
    kv_send,
    kv_recv,
    z_send,
    z_recv,
    o_send,
    o_recv,
):
    heads, _, _, block, head_size = kv_buf.shape
    rows = block // 2
    group = lax.axis_index("groups")
    position = lax.axis_index("outer") * inner + lax.axis_index("inner")
    side = lax.rem(position, 2)
    has_below = position >= 2
    has_above = position < positions - 2

    def at(where):
        return (group, where // inner, lax.rem(where, inner))

    partner = at(position + 1 - 2 * side)
    below = at(jnp.maximum(position - 2, 0))
    above = at(jnp.minimum(position + 2, positions - 1))
    own_rows = pl.ds(pl.multiple_of(side * rows, rows), rows)
    partner_rows = pl.ds(pl.multiple_of((1 - side) * rows, rows), rows)

    def columns(which_side, head):
        return pl.ds(pl.multiple_of((which_side * heads + head) * head_size, head_size), head_size)

    def remote(src, dst, send, recv, target):
        return pltpu.make_async_remote_copy(
            src_ref=src, dst_ref=dst, send_sem=send, recv_sem=recv, device_id=target, device_id_type=MESH
        )

    def q_pair(head, which_rows):
        return remote(
            q_ref.at[:, columns(1 - side, head)],
            q_buf.at[head, which_rows],
            q_send.at[head],
            q_recv.at[head],
            partner,
        )

    def kv_pair(head, which_rows):
        return remote(
            kv_ref.at[:, :, columns(1 - side, head)],
            kv_buf.at[head, OWN, :, which_rows],
            kv_send.at[head],
            kv_recv.at[head],
            partner,
        )

    def q_keep(head):
        return pltpu.make_async_copy(
            q_ref.at[:, columns(side, head)], q_buf.at[head, own_rows], q_local.at[head]
        )

    def kv_keep(head):
        return pltpu.make_async_copy(
            kv_ref.at[:, :, columns(side, head)], kv_buf.at[head, OWN, :, own_rows], kv_local.at[head]
        )

    def own_along(head, part, up):
        return remote(
            kv_ref.at[part, :, columns(side, head)],
            kv_buf.at[head, BELOW if up else ABOVE, part, own_rows],
            z_send.at[int(up), 0, part, head],
            z_recv.at[int(up), 0, part, head],
            above if up else below,
        )

    def passed_along(head, part, up):
        return remote(
            kv_buf.at[head, OWN, part, partner_rows],
            kv_buf.at[head, BELOW if up else ABOVE, part, partner_rows],
            z_send.at[int(up), 1, part, head],
            z_recv.at[int(up), 1, part, head],
            above if up else below,
        )

    def both_ways(act):
        @pl.when(has_above)
        def _():
            act(True)

        @pl.when(has_below)
        def _():
            act(False)

    def wait_along(head, part):
        @pl.when(has_below)
        def _():
            own_along(head, part, True).wait_recv()
            passed_along(head, part, True).wait_recv()

        @pl.when(has_above)
        def _():
            own_along(head, part, False).wait_recv()
            passed_along(head, part, False).wait_recv()

    def out_pair(head, which_side):
        return remote(
            o_buf.at[head, partner_rows],
            out_ref.at[:, columns(which_side, head)],
            o_send.at[head],
            o_recv.at[head],
            partner,
        )

    def out_keep(head):
        return pltpu.make_async_copy(
            o_buf.at[head, own_rows], out_ref.at[:, columns(side, head)], o_local.at[head]
        )

    def each_head(body):
        lax.fori_loop(0, heads, lambda head, carry: (body(head), carry)[1], 0)

    barrier = pltpu.get_barrier_semaphore()
    pl.semaphore_signal(barrier, inc=1, device_id=partner, device_id_type=MESH)

    @pl.when(has_below)
    def _():
        pl.semaphore_signal(barrier, inc=1, device_id=below, device_id_type=MESH)

    @pl.when(has_above)
    def _():
        pl.semaphore_signal(barrier, inc=1, device_id=above, device_id_type=MESH)

    table_keep = pltpu.make_async_copy(table_hbm, table_ref, table_local)
    bias_keep = pltpu.make_async_copy(bias_hbm, bias_ref, bias_local)
    table_keep.start()
    bias_keep.start()

    def start_keep(head):
        q_keep(head).start()
        kv_keep(head).start()

    each_head(start_keep)

    pl.semaphore_wait(barrier, 1 + has_below.astype(jnp.int32) + has_above.astype(jnp.int32))

    def start_pair(head):
        kv_pair(head, own_rows).start()
        q_pair(head, own_rows).start()

    def start_own(head, part):
        both_ways(lambda up: own_along(head, part, up).start())

    def start_passed(head, part):
        both_ways(lambda up: passed_along(head, part, up).start())

    for head in range(ALONG_AHEAD):
        start_own(head, 0)
        start_pair(head)
        start_own(head, 1)
    for head in range(ALONG_AHEAD, PAIR_AHEAD):
        start_pair(head)

    @pl.when(jnp.logical_not(has_below))
    def _():
        each_head(lambda head: kv_buf.__setitem__((head, BELOW), jnp.zeros((2, block, head_size), kv_buf.dtype)))

    @pl.when(jnp.logical_not(has_above))
    def _():
        each_head(lambda head: kv_buf.__setitem__((head, ABOVE), jnp.zeros((2, block, head_size), kv_buf.dtype)))

    for head in range(ALONG_AHEAD):
        kv_pair(head, partner_rows).wait_recv()
        start_passed(head, 0)
        start_passed(head, 1)
    table_keep.wait()
    bias_keep.wait()

    block_index = position // 2
    last_block = positions // 2 - 1
    scale = LOG2E / math.sqrt(head_size)

    def key_bias(head, slot):
        key_block = jnp.clip(block_index + slot - 1, 0, last_block)
        region = table_ref[block_index, key_block]
        live = region > 0
        if slot == BELOW:
            live = live & has_below
        if slot == ABOVE:
            live = live & has_above
        return jnp.where(live, bias_ref[side * heads + head, region] * LOG2E, DEAD)

    def finish_sends(head):
        q_pair(head, own_rows).wait_send()
        kv_pair(head, own_rows).wait_send()
        for part in range(2):
            both_ways(lambda up: own_along(head, part, up).wait_send())
            both_ways(lambda up: passed_along(head, part, up).wait_send())

    def finish(head):
        out_keep(head).wait()
        out_pair(head, side).wait_send()
        out_pair(head, 1 - side).wait_recv()

    def attend(head):
        q_pair(head, partner_rows).wait_recv()
        q_keep(head).wait()
        kv_keep(head).wait()
        wait_along(head, 0)

        @pl.when(head + ALONG_AHEAD < heads)
        def _():
            kv_pair(head + ALONG_AHEAD, partner_rows).wait_recv()
            start_own(head + ALONG_AHEAD, 0)
            start_passed(head + ALONG_AHEAD, 0)
            start_own(head + ALONG_AHEAD, 1)
            start_passed(head + ALONG_AHEAD, 1)

        @pl.when(head + PAIR_AHEAD < heads)
        def _():
            start_pair(head + PAIR_AHEAD)

        @pl.when(head >= FINISH_BEHIND)
        def _():
            finish_sends(head - FINISH_BEHIND)
            finish(head - FINISH_BEHIND)

        slots = (BELOW, OWN, ABOVE)
        biases = [key_bias(head, slot) for slot in slots]
        totals = []
        for half, tile in enumerate((partner_rows, own_rows)):
            query = q_buf[head, tile]
            products = [
                lax.dot_general(
                    query, kv_buf[head, slot, 0], (((1,), (1,)), ((), ())), preferred_element_type=jnp.float32
                )
                for slot in slots
            ]
            peak = functools.reduce(
                jnp.maximum,
                [jnp.max(scores, axis=1, keepdims=True) * scale + bias for scores, bias in zip(products, biases)],
            )
            total = jnp.zeros((rows, 1), jnp.float32)
            for slot in slots:
                weights = jnp.exp2(products[slot] * scale + (biases[slot] - peak))
                total = total + jnp.sum(weights, axis=1, keepdims=True)
                w_buf[half, slot] = weights.astype(w_buf.dtype)
            totals.append(total)
        wait_along(head, 1)
        for half, tile in enumerate((partner_rows, own_rows)):
            weighted = jnp.zeros((rows, head_size), jnp.float32)
            for slot in slots:
                weighted = weighted + jnp.dot(
                    w_buf[half, slot], kv_buf[head, slot, 1], preferred_element_type=jnp.float32
                )
            o_buf[head, tile] = (weighted / totals[half]).astype(o_buf.dtype)
            if half == 0:
                out_pair(head, side).start()
        out_keep(head).start()

    each_head(attend)

    for head in range(heads - FINISH_BEHIND, heads):
        finish_sends(head)
    for head in range(heads - FINISH_BEHIND, heads):
        finish(head)


def per_device(inner, positions, queries, key_value, region_table, region_bias):
    tokens, feature_width = queries.shape
    head_count = region_bias.shape[0]
    head_size = feature_width // head_count
    heads = head_count // 2
    block = 2 * tokens
    dma = pltpu.SemaphoreType.DMA
    return pl.pallas_call(
        functools.partial(kernel, inner, positions),
        out_shape=jax.ShapeDtypeStruct((tokens, feature_width), jnp.bfloat16),
        in_specs=[
            pl.BlockSpec(memory_space=pl.ANY),
            pl.BlockSpec(memory_space=pl.ANY),
            pl.BlockSpec(memory_space=pl.ANY),
            pl.BlockSpec(memory_space=pl.ANY),
        ],
        out_specs=pl.BlockSpec(memory_space=pl.ANY),
        scratch_shapes=[
            pltpu.SMEM(region_table.shape, region_table.dtype),
            pltpu.SMEM(region_bias.shape, region_bias.dtype),
            pltpu.VMEM((heads, block, head_size), jnp.bfloat16),
            pltpu.VMEM((heads, 3, 2, block, head_size), jnp.bfloat16),
            pltpu.VMEM((heads, block, head_size), jnp.bfloat16),
            pltpu.VMEM((2, 3, tokens, block), jnp.bfloat16),
            dma,
            dma,
            dma((heads,)),
            dma((heads,)),
            dma((heads,)),
            dma((heads,)),
            dma((heads,)),
            dma((heads,)),
            dma((heads,)),
            dma((2, 2, 2, heads)),
            dma((2, 2, 2, heads)),
            dma((heads,)),
            dma((heads,)),
        ],
        compiler_params=pltpu.CompilerParams(
            collective_id=0, has_side_effects=True, vmem_limit_bytes=60 * 1024 * 1024
        ),
    )(region_table, region_bias, queries, key_value)


def solution(mesh):
    inner = mesh.shape["inner"]
    positions = mesh.shape["outer"] * inner
    placed = (
        P(("groups", "outer", "inner"), None),
        P(None, ("groups", "outer", "inner"), None),
        P("groups", None),
        P(),
    )
    return jax.shard_map(
        functools.partial(per_device, inner, positions),
        mesh=mesh,
        in_specs=placed,
        out_specs=P(("groups", "outer", "inner"), None),
        check_vma=False,
    )
```

```python
import functools
import math

import jax
import jax.numpy as jnp
from jax import lax
from jax.experimental import pallas as pl
from jax.experimental.pallas import tpu as pltpu
from jax.sharding import PartitionSpec as P

MESH = pl.DeviceIdType.MESH
BELOW, OWN, ABOVE = 0, 1, 2
LOG2E = math.log2(math.e)
DEAD = -1e30
ALONG_AHEAD = 2
PAIR_AHEAD = 4
FINISH_BEHIND = 3


def kernel(
    inner,
    positions,
    table_hbm,
    bias_hbm,
    q_ref,
    kv_ref,
    out_ref,
    table_ref,
    bias_ref,
    q_buf,
    kv_buf,
    o_buf,
    w_buf,
    table_local,
    bias_local,
    q_local,
    kv_local,
    o_local,
    q_send,
    q_recv,
    kv_send,
    kv_recv,
    z_send,
    z_recv,
    o_send,
    o_recv,
):
    heads, _, _, block, head_size = kv_buf.shape
    rows = block // 2
    group = lax.axis_index("groups")
    position = lax.axis_index("outer") * inner + lax.axis_index("inner")
    side = lax.rem(position, 2)
    has_below = position >= 2
    has_above = position < positions - 2

    def at(where):
        return (group, where // inner, lax.rem(where, inner))

    partner = at(position + 1 - 2 * side)
    below = at(jnp.maximum(position - 2, 0))
    above = at(jnp.minimum(position + 2, positions - 1))
    own_rows = pl.ds(pl.multiple_of(side * rows, rows), rows)
    partner_rows = pl.ds(pl.multiple_of((1 - side) * rows, rows), rows)

    def columns(which_side, head):
        return pl.ds(pl.multiple_of((which_side * heads + head) * head_size, head_size), head_size)

    def remote(src, dst, send, recv, target):
        return pltpu.make_async_remote_copy(
            src_ref=src, dst_ref=dst, send_sem=send, recv_sem=recv, device_id=target, device_id_type=MESH
        )

    def q_pair(head, which_rows):
        return remote(
            q_ref.at[:, columns(1 - side, head)],
            q_buf.at[head, which_rows],
            q_send.at[head],
            q_recv.at[head],
            partner,
        )

    def kv_pair(head, which_rows):
        return remote(
            kv_ref.at[:, :, columns(1 - side, head)],
            kv_buf.at[head, OWN, :, which_rows],
            kv_send.at[head],
            kv_recv.at[head],
            partner,
        )

    def q_keep(head):
        return pltpu.make_async_copy(
            q_ref.at[:, columns(side, head)], q_buf.at[head, own_rows], q_local.at[head]
        )

    def kv_keep(head):
        return pltpu.make_async_copy(
            kv_ref.at[:, :, columns(side, head)], kv_buf.at[head, OWN, :, own_rows], kv_local.at[head]
        )

    def own_along(head, part, up):
        return remote(
            kv_ref.at[part, :, columns(side, head)],
            kv_buf.at[head, BELOW if up else ABOVE, part, own_rows],
            z_send.at[int(up), 0, part, head],
            z_recv.at[int(up), 0, part, head],
            above if up else below,
        )

    def passed_along(head, part, up):
        return remote(
            kv_buf.at[head, OWN, part, partner_rows],
            kv_buf.at[head, BELOW if up else ABOVE, part, partner_rows],
            z_send.at[int(up), 1, part, head],
            z_recv.at[int(up), 1, part, head],
            above if up else below,
        )

    def both_ways(act):
        @pl.when(has_above)
        def _():
            act(True)

        @pl.when(has_below)
        def _():
            act(False)

    def wait_along(head, part):
        @pl.when(has_below)
        def _():
            own_along(head, part, True).wait_recv()
            passed_along(head, part, True).wait_recv()

        @pl.when(has_above)
        def _():
            own_along(head, part, False).wait_recv()
            passed_along(head, part, False).wait_recv()

    def out_pair(head, which_side):
        return remote(
            o_buf.at[head, partner_rows],
            out_ref.at[:, columns(which_side, head)],
            o_send.at[head],
            o_recv.at[head],
            partner,
        )

    def out_keep(head):
        return pltpu.make_async_copy(
            o_buf.at[head, own_rows], out_ref.at[:, columns(side, head)], o_local.at[head]
        )

    def each_head(body):
        lax.fori_loop(0, heads, lambda head, carry: (body(head), carry)[1], 0)

    barrier = pltpu.get_barrier_semaphore()
    pl.semaphore_signal(barrier, inc=1, device_id=partner, device_id_type=MESH)

    @pl.when(has_below)
    def _():
        pl.semaphore_signal(barrier, inc=1, device_id=below, device_id_type=MESH)

    @pl.when(has_above)
    def _():
        pl.semaphore_signal(barrier, inc=1, device_id=above, device_id_type=MESH)

    table_keep = pltpu.make_async_copy(table_hbm, table_ref, table_local)
    bias_keep = pltpu.make_async_copy(bias_hbm, bias_ref, bias_local)
    table_keep.start()
    bias_keep.start()

    def start_keep(head):
        q_keep(head).start()
        kv_keep(head).start()

    each_head(start_keep)

    pl.semaphore_wait(barrier, 1 + has_below.astype(jnp.int32) + has_above.astype(jnp.int32))

    def start_pair(head):
        kv_pair(head, own_rows).start()
        q_pair(head, own_rows).start()

    def start_own(head, part):
        both_ways(lambda up: own_along(head, part, up).start())

    def start_passed(head, part):
        both_ways(lambda up: passed_along(head, part, up).start())

    for head in range(ALONG_AHEAD):
        start_own(head, 0)
        start_pair(head)
        start_own(head, 1)
    for head in range(ALONG_AHEAD, PAIR_AHEAD):
        start_pair(head)

    @pl.when(jnp.logical_not(has_below))
    def _():
        each_head(lambda head: kv_buf.__setitem__((head, BELOW), jnp.zeros((2, block, head_size), kv_buf.dtype)))

    @pl.when(jnp.logical_not(has_above))
    def _():
        each_head(lambda head: kv_buf.__setitem__((head, ABOVE), jnp.zeros((2, block, head_size), kv_buf.dtype)))

    for head in range(ALONG_AHEAD):
        kv_pair(head, partner_rows).wait_recv()
        start_passed(head, 0)
        start_passed(head, 1)
    table_keep.wait()
    bias_keep.wait()

    block_index = position // 2
    last_block = positions // 2 - 1
    scale = LOG2E / math.sqrt(head_size)

    def key_bias(head, slot):
        key_block = jnp.clip(block_index + slot - 1, 0, last_block)
        region = table_ref[block_index, key_block]
        live = region > 0
        if slot == BELOW:
            live = live & has_below
        if slot == ABOVE:
            live = live & has_above
        return jnp.where(live, bias_ref[side * heads + head, region] * LOG2E, DEAD)

    def finish_sends(head):
        q_pair(head, own_rows).wait_send()
        kv_pair(head, own_rows).wait_send()
        for part in range(2):
            both_ways(lambda up: own_along(head, part, up).wait_send())
            both_ways(lambda up: passed_along(head, part, up).wait_send())

    def finish(head):
        out_keep(head).wait()
        out_pair(head, side).wait_send()
        out_pair(head, 1 - side).wait_recv()

    def attend(head):
        q_pair(head, partner_rows).wait_recv()
        q_keep(head).wait()
        kv_keep(head).wait()
        wait_along(head, 0)

        @pl.when(head + ALONG_AHEAD < heads)
        def _():
            kv_pair(head + ALONG_AHEAD, partner_rows).wait_recv()
            start_own(head + ALONG_AHEAD, 0)
            start_passed(head + ALONG_AHEAD, 0)
            start_own(head + ALONG_AHEAD, 1)
            start_passed(head + ALONG_AHEAD, 1)

        @pl.when(head + PAIR_AHEAD < heads)
        def _():
            start_pair(head + PAIR_AHEAD)

        @pl.when(head >= FINISH_BEHIND)
        def _():
            finish_sends(head - FINISH_BEHIND)
            finish(head - FINISH_BEHIND)

        slots = (BELOW, OWN, ABOVE)
        biases = [key_bias(head, slot) for slot in slots]
        totals = []
        for half, tile in enumerate((partner_rows, own_rows)):
            query = q_buf[head, tile]
            products = [
                lax.dot_general(
                    query, kv_buf[head, slot, 0], (((1,), (1,)), ((), ())), preferred_element_type=jnp.float32
                )
                for slot in slots
            ]
            peak = functools.reduce(
                jnp.maximum,
                [jnp.max(scores, axis=1, keepdims=True) * scale + bias for scores, bias in zip(products, biases)],
            )
            total = jnp.zeros((rows, 1), jnp.float32)
            for slot in slots:
                weights = jnp.exp2(products[slot] * scale + (biases[slot] - peak))
                total = total + jnp.sum(weights, axis=1, keepdims=True)
                w_buf[half, slot] = weights.astype(w_buf.dtype)
            totals.append(total)
        started = [
            jnp.dot(w_buf[half, OWN], kv_buf[head, OWN, 1], preferred_element_type=jnp.float32)
            for half in range(2)
        ]
        wait_along(head, 1)
        for half, tile in enumerate((partner_rows, own_rows)):
            weighted = started[half]
            for slot in (BELOW, ABOVE):
                weighted = weighted + jnp.dot(
                    w_buf[half, slot], kv_buf[head, slot, 1], preferred_element_type=jnp.float32
                )
            o_buf[head, tile] = (weighted / totals[half]).astype(o_buf.dtype)
            if half == 0:
                out_pair(head, side).start()
        out_keep(head).start()

    each_head(attend)

    for head in range(heads - FINISH_BEHIND, heads):
        finish_sends(head)
    for head in range(heads - FINISH_BEHIND, heads):
        finish(head)


def per_device(inner, positions, queries, key_value, region_table, region_bias):
    tokens, feature_width = queries.shape
    head_count = region_bias.shape[0]
    head_size = feature_width // head_count
    heads = head_count // 2
    block = 2 * tokens
    dma = pltpu.SemaphoreType.DMA
    return pl.pallas_call(
        functools.partial(kernel, inner, positions),
        out_shape=jax.ShapeDtypeStruct((tokens, feature_width), jnp.bfloat16),
        in_specs=[
            pl.BlockSpec(memory_space=pl.ANY),
            pl.BlockSpec(memory_space=pl.ANY),
            pl.BlockSpec(memory_space=pl.ANY),
            pl.BlockSpec(memory_space=pl.ANY),
        ],
        out_specs=pl.BlockSpec(memory_space=pl.ANY),
        scratch_shapes=[
            pltpu.SMEM(region_table.shape, region_table.dtype),
            pltpu.SMEM(region_bias.shape, region_bias.dtype),
            pltpu.VMEM((heads, block, head_size), jnp.bfloat16),
            pltpu.VMEM((heads, 3, 2, block, head_size), jnp.bfloat16),
            pltpu.VMEM((heads, block, head_size), jnp.bfloat16),
            pltpu.VMEM((2, 3, tokens, block), jnp.bfloat16),
            dma,
            dma,
            dma((heads,)),
            dma((heads,)),
            dma((heads,)),
            dma((heads,)),
            dma((heads,)),
            dma((heads,)),
            dma((heads,)),
            dma((2, 2, 2, heads)),
            dma((2, 2, 2, heads)),
            dma((heads,)),
            dma((heads,)),
        ],
        compiler_params=pltpu.CompilerParams(
            collective_id=0, has_side_effects=True, vmem_limit_bytes=60 * 1024 * 1024
        ),
    )(region_table, region_bias, queries, key_value)


def solution(mesh):
    inner = mesh.shape["inner"]
    positions = mesh.shape["outer"] * inner
    placed = (
        P(("groups", "outer", "inner"), None),
        P(None, ("groups", "outer", "inner"), None),
        P("groups", None),
        P(),
    )
    return jax.shard_map(
        functools.partial(per_device, inner, positions),
        mesh=mesh,
        in_specs=placed,
        out_specs=P(("groups", "outer", "inner"), None),
        check_vma=False,
    )
```
